32 devices in a mesh: group: 1, shard: 32 (over z, y, x, core).
Axes of the slice: x: 2, y: 2, z: 4, core: 2. Of those that a mesh axis runs over, the one named last changes fastest.
Arguments:
- activations: bfloat16 [64, 256, 4096], P(('group', 'shard')), may hold values from -6 to 6
- out_grads: bfloat16 [64, 256, 1024], P(('group', 'shard')), may hold values from -6 to 6
- value_weight: bfloat16 [4096, 1024], P('shard'), may hold values from -0.09375 to 0.09375
- basis_in: bfloat16 [4096, 64], replicated, may hold values from -0.09375 to 0.09375
- basis_out: bfloat16 [1024, 64], replicated, may hold values from -0.1875 to 0.1875
- doc_lengths: int32 [64], P(('group', 'shard')), may hold values from 1 to 256, 12288 in all
- queries: bfloat16 [1024, 4096], P('shard'), may hold values from -0.005859375 to 0.005859375
Outputs:
- input_grad: bfloat16 [64, 256, 4096], P(('group', 'shard'))
- scores: float32 [1024, 64], P('shard', 'group')
The draws below stay inside these ranges and needn't reach their ends.
All inputs are finite; a program needn't handle non-finite values. No bound on the sum of `doc_lengths` on one device may be relied on, other than what follows from the above.
Results may differ from the reference program's by a relative error of at most 0.0058.
Values may be sent and summed in bfloat16 or wider, within the bound.
A program may use at most 64 MiB of HBM per device.

```python
import math
import jax
import jax.numpy as jnp
import numpy as np
from jax import lax

D = 4096
KV = 1024
R = 64
LENGTH = 256
DOCS = 64
QUERIES = 1024


def block_levels(key, dims, split, smallest, largest):
    factor_of, own = 1.0, jax.random.fold_in(key, 6)
    for axis_at, shards_of in split:
        heights = jnp.exp(jax.random.uniform(jax.random.fold_in(own, axis_at), (shards_of,), jnp.float32, smallest / len(split), largest / len(split)))
        factor_of = factor_of * jnp.repeat(heights, dims[axis_at] // shards_of).reshape([-1 if axis == axis_at else 1 for axis in range(len(dims))])
    return factor_of


def length_profile(count, total, limit, lean):
    loads = [(1 << 20) // math.isqrt(rank ** lean) + 1 for rank in range(2, count + 1)]
    surplus, holding = total - limit - (count - 1), [1] * (count - 1)
    while surplus > 0:
        movable = [i for i in range(count - 1) if holding[i] < limit]
        whole, left = sum([loads[i] for i in movable]), surplus
        for i in movable:
            extra = min(limit - holding[i], max(1, left * loads[i] // whole), surplus)
            holding[i] = holding[i] + extra
            surplus = surplus - extra
    return np.array([limit] + holding)


def uneven_parts(own_key, amount, total, most, skew):
    if amount == 2:
        one = jax.random.randint(own_key, (), max(1, total - most), min(most, total - 1) + 1)
        return jnp.stack([one, total - one])
    sizes = jnp.asarray(length_profile(amount, total, most, skew), jnp.int32)
    pairs = (amount - 1) // 2
    donor, receiver = sizes[1:1 + 2 * pairs:2], sizes[2:2 + 2 * pairs:2]
    room = jnp.minimum(donor - 1, most - receiver)
    shifted = jax.random.randint(jax.random.fold_in(own_key, 1), (pairs,), 0, 1 << 20) % (room + 1)
    sizes = sizes.at[1:1 + 2 * pairs:2].set(donor - shifted).at[2:2 + 2 * pairs:2].set(receiver + shifted)
    return sizes[jax.random.permutation(jax.random.fold_in(own_key, 2), amount)]


def normal_values(rng, dims, scale, reach, pieces=(), kind=jnp.bfloat16):
    array = jax.random.normal(rng, dims, jnp.float32) * scale
    if len(pieces) > 0:
        array = block_levels(rng, dims, pieces, -0.22, 0.18) * array
    return jnp.clip(array, min=-reach, max=reach).astype(kind)


def setup_inputs(seed: int = 0, part: int = 0) -> dict:
    keys = jax.random.split(jax.random.key(seed), 8)
    own_keys = jax.random.split(jax.random.fold_in(keys[7], part), 8)
    activations = normal_values(own_keys[0], (DOCS, LENGTH, D), 1.0, 6.0, ((0, 32),))
    out_grads = normal_values(own_keys[1], (DOCS, LENGTH, KV), 1.0, 6.0, ((0, 32),))
    value_weight = normal_values(keys[2], (D, KV), D ** -0.5, 0.09375, ((0, 32),))
    basis_in = normal_values(keys[3], (D, R), D ** -0.5, 0.09375)
    basis_out = normal_values(keys[4], (KV, R), KV ** -0.5, 0.1875)
    doc_lengths = uneven_parts(own_keys[5], DOCS, 3 * DOCS * LENGTH // 4, LENGTH, 1).astype(jnp.int32)
    queries = normal_values(keys[6], (QUERIES, R * R), (R * R * LENGTH) ** -0.5, 0.005859375, ((0, 32),))
    return {"activations": activations, "out_grads": out_grads, "value_weight": value_weight, "basis_in": basis_in, "basis_out": basis_out, "doc_lengths": doc_lengths, "queries": queries}


def reference(activations, out_grads, value_weight, basis_in, basis_out, doc_lengths, queries):
    docs = activations.shape[0]
    positions = jnp.arange(LENGTH, dtype=jnp.int32)
    valid = (positions[None, :] < doc_lengths[:, None]).astype(jnp.float32)

    def one_doc(pair):
        grads, keep = pair
        full = jnp.dot(grads, value_weight.T, preferred_element_type=jnp.float32)
        return (full * keep[:, None]).astype(jnp.bfloat16)

    input_grad = lax.map(one_doc, (out_grads, valid))
    reduced_in = jnp.dot(activations.reshape(-1, D), basis_in, preferred_element_type=jnp.float32)
    reduced_in = reduced_in.astype(jnp.bfloat16).reshape(docs, LENGTH, R)
    reduced_out = jnp.dot(out_grads.reshape(-1, KV), basis_out, preferred_element_type=jnp.float32)
    reduced_out = (reduced_out.reshape(docs, LENGTH, R) * valid[:, :, None]).astype(jnp.bfloat16)
    projected = jnp.einsum("dti,dto->dio", reduced_in.astype(jnp.float32), reduced_out.astype(jnp.float32))
    projected = projected.astype(jnp.bfloat16).reshape(docs, R * R)
    scores = jnp.dot(queries, projected.T, preferred_element_type=jnp.float32)
    return input_grad, scores
```

```python
import functools

import jax
import jax.numpy as jnp
from jax import lax
from jax.experimental import pallas as pl
from jax.experimental.pallas import tpu as pltpu
from jax.sharding import PartitionSpec as P

LINK_X, LINK_Y, LINK_CORE = 0, 1, 2
PARTS = 3


def kernel(
    dims, wrap, lengths, act_hbm, grads_hbm, own_hbm, basis_in_hbm, basis_out_hbm, queries_hbm,
    out_hbm, scores_ref,
    weight, projected, act, grads, basis_in, basis_out, queries, staged, gram, wide, flat,
    load_sem, recv_sem, along_sem, link_sem, out_sem,
):
    depth, height, width = dims
    chips = depth * height * width
    me = lax.axis_index("shard")
    core = lax.rem(me, 2)
    x = lax.rem(lax.div(me, 2), width)
    y = lax.rem(lax.div(me, 2 * width), height)
    z = lax.div(me, 2 * width * height)
    rows = own_hbm.shape[0]
    half = rows // 2
    docs = lengths.shape[0]
    length = grads.shape[0] // docs
    rank = basis_in.shape[1]
    packed = projected.shape[0] // (2 * chips)
    per_doc = packed // docs
    plane = width > 1
    reach = depth // 2 + 1 if wrap else depth

    def index(at_z, at_y, at_x, at_core):
        return ((at_z * height + at_y) * width + at_x) * 2 + at_core

    def device(shard):
        return {"shard": shard}

    sibling = index(z, y, x, 1 - core)
    beside_x = index(z, y, 1 - x, core) if plane else None
    beside_y = index(z, 1 - y, x, core) if plane else None

    def at(side, far):
        return lax.rem(z + side * far + depth, depth) if wrap else z + side * far

    def exists(side, far):
        if wrap:
            last = depth // 2 if side > 0 else (depth - 1) // 2
            return (far >= (0 if side > 0 else 1)) & (far <= last)
        if side > 0:
            return (far >= 0) & (z + far < depth)
        return (far >= 1) & (z - far >= 0)

    def goes_on(side, far):
        if wrap:
            return far + 1 <= (depth // 2 if side > 0 else (depth - 1) // 2)
        return z > 0 if side > 0 else z < depth - 1

    def place(shard, part):
        if part == 2:
            return projected.at[pl.ds(pl.multiple_of(shard * packed, packed), packed)]
        return weight.at[pl.ds(pl.multiple_of(shard * rows + part * half, half), half)]

    def copy(shard, part, to, send_sem, source=None):
        target = place(shard, part)
        return pltpu.make_async_remote_copy(
            src_ref=target if source is None else source,
            dst_ref=target,
            send_sem=send_sem,
            recv_sem=recv_sem.at[shard * PARTS + part],
            device_id=device(to),
            device_id_type=pl.DeviceIdType.MESH,
        )

    def link(which, part):
        return link_sem.at[which * 2 + (1 if part == 2 else 0)]

    def arrived(shard, part):
        copy(shard, part, sibling, link(LINK_CORE, part)).wait_recv()

    def along(side, far, part):
        return along_sem.at[((0 if side > 0 else 1) * reach + far) * PARTS + part]

    def send_along(side, far, shard, part, source=None):
        @pl.when(goes_on(side, far))
        def _():
            copy(shard, part, index(at(-side, 1), y, x, core), along(side, far, part), source).start()

    def send_x(shard, part, source=None):
        if plane:
            copy(shard, part, beside_x, link(LINK_X, part), source).start()

    def send_y(shard, part, source=None):
        if plane:
            copy(shard, part, beside_y, link(LINK_Y, part), source).start()

    def send_core(shard, part, source=None):
        copy(shard, part, sibling, link(LINK_CORE, part), source).start()

    own = weight.at[pl.ds(pl.multiple_of(me * rows, rows), rows)]
    loads = [
        pltpu.make_async_copy(source, target, load_sem.at[i])
        for i, (source, target) in enumerate(
            [
                (grads_hbm, grads),
                (basis_out_hbm, basis_out),
                (basis_in_hbm, basis_in),
                (act_hbm, act),
                (own_hbm, own),
                (queries_hbm, queries),
            ]
        )
    ]
    for load in loads:
        load.start()

    barrier = pltpu.get_barrier_semaphore()

    def greet(other):
        pl.semaphore_signal(barrier, inc=1, device_id=device(other), device_id_type=pl.DeviceIdType.MESH)

    greet(sibling)
    if plane:
        greet(beside_x)
        greet(beside_y)
    partners = 3 if plane else 1
    if wrap:
        greet(index(at(1, 1), y, x, core))
        greet(index(at(-1, 1), y, x, core))
        pl.semaphore_wait(barrier, partners + 2)
    else:
        @pl.when(z + 1 < depth)
        def _():
            greet(index(z + 1, y, x, core))

        @pl.when(z > 0)
        def _():
            greet(index(z - 1, y, x, core))

        pl.semaphore_wait(
            barrier, partners + jnp.where(z + 1 < depth, 1, 0) + jnp.where(z > 0, 1, 0)
        )

    for part in range(2):
        source = own_hbm.at[pl.ds(part * half, half)]
        for side in (1, -1):
            send_along(side, 0, me, part, source)
        send_x(me, part, source)
        send_y(me, part, source)
        send_core(me, part, source)

    for load in loads[:4]:
        load.wait()

    @pl.loop(0, docs)
    def _(doc):
        tokens = pl.ds(pl.multiple_of(doc * length, length), length)
        token = lax.broadcasted_iota(jnp.int32, (length, grads.shape[1]), 0)
        valid = (token < lengths[doc]).astype(jnp.float32)
        grads[tokens, :] = (grads[tokens, :].astype(jnp.float32) * valid).astype(jnp.bfloat16)
        reduced_in = jnp.dot(
            act[tokens, :], basis_in[...], preferred_element_type=jnp.float32
        ).astype(jnp.bfloat16)
        reduced_out = jnp.dot(grads[tokens, :], basis_out[...], preferred_element_type=jnp.float32)
        both = jnp.concatenate([reduced_out, reduced_out], axis=1).astype(jnp.bfloat16)
        gram[...] = lax.dot_general(
            reduced_in, both, (((0,), (0,)), ((), ())), preferred_element_type=jnp.float32
        )
        even = gram[pl.ds(0, per_doc, stride=2), :]
        odd = gram[pl.ds(1, per_doc, stride=2), :]
        lane = lax.broadcasted_iota(jnp.int32, (per_doc, 2 * rank), 1)
        projected[pl.ds(pl.multiple_of(me * packed + doc * per_doc, per_doc), per_doc), :] = (
            jnp.where(lane < rank, even, odd).astype(jnp.bfloat16)
        )

    for side in (1, -1):
        send_along(side, 0, me, 2)
    send_x(me, 2)
    send_y(me, 2)
    send_core(me, 2)
    loads[4].wait()
    loads[5].wait()

    def pass_on(step):
        for part in range(PARTS):
            for side in (1, -1):
                @pl.when(exists(side, step))
                def _(side=side):
                    shard = index(at(side, step), y, x, core)
                    arrived(shard, part)
                    send_along(side, step, shard, part)
                    send_x(shard, part)
                    send_y(shard, part)
                    send_core(shard, part)

                if plane:
                    @pl.when(exists(side, step - 1))
                    def _(side=side):
                        level = at(side, step - 1)
                        shard = index(level, y, 1 - x, core)
                        arrived(shard, part)
                        if part == 1:
                            send_y(shard, part)
                        send_core(shard, part)
                        shard = index(level, 1 - y, x, core)
                        arrived(shard, part)
                        if part != 1:
                            send_x(shard, part)
                        send_core(shard, part)

                    @pl.when(exists(side, step - 2))
                    def _(side=side):
                        shard = index(at(side, step - 2), 1 - y, 1 - x, core)
                        arrived(shard, part)
                        send_core(shard, part)

    def multiply(chip):
        for part in range(2):
            arrived(chip * 2 + 1 - core, part)
        block = weight[pl.ds(pl.multiple_of(chip * 2 * rows, 2 * rows), 2 * rows), :]
        columns = pl.ds(pl.multiple_of(chip * 2 * rows, 2 * rows), 2 * rows)
        staged[:, columns] = lax.dot_general(
            grads[...], block, (((1,), (1,)), ((), ())), preferred_element_type=jnp.float32
        ).astype(jnp.bfloat16)
        pltpu.make_async_copy(staged.at[:, columns], out_hbm.at[:, columns], out_sem.at[0]).start()

    def work(step):
        @pl.loop(0, 2 * height * width)
        def _(turn):
            column = lax.div(turn, 2)
            turned = lax.rem(turn, 2)
            off_x = lax.rem(column, 2) if plane else 0
            off_y = lax.div(column, 2) if plane else 0
            far = step - 1 - off_x - off_y
            up = exists(1, far) & (turned == 0)
            down = exists(-1, far) & (turned == 1)
            at_x = x + off_x - 2 * x * off_x
            at_y = y + off_y - 2 * y * off_y
            level = at(1 - 2 * turned, far)

            @pl.when(up | down)
            def _():
                multiply((level * height + at_y) * width + at_x)

    last = reach - 1 + (2 if plane else 0)

    @pl.loop(1, last + 1)
    def _(step):
        pass_on(step)
        work(step)

    @pl.loop(0, chips)
    def _(chip):
        arrived(chip * 2 + 1 - core, 2)

    wide[...] = projected[...].astype(jnp.float32)
    for k in range(per_doc):
        flat[:, k * 2 * rank : (k + 1) * 2 * rank] = wide[
            pl.ds(k, 2 * chips * docs, stride=per_doc), :
        ].astype(jnp.bfloat16)
    scores_ref[...] = lax.dot_general(
        queries[...], flat[...], (((1,), (1,)), ((), ())), preferred_element_type=jnp.float32
    )
    work(last + 1)

    for side in (1, -1):
        @pl.loop(0, reach)
        def _(far, side=side):
            @pl.when((exists(side, far) | (far == 0)) & goes_on(side, far))
            def _():
                shard = index(at(side, far), y, x, core)
                for part in range(PARTS):
                    copy(shard, part, sibling, along(side, far, part)).wait_send()

    def all_sent(which, weight_rows, packed_rows):
        for part, ref, size in ((0, weight, weight_rows), (2, projected, packed_rows)):
            whole = ref.at[pl.ds(0, size)]
            pltpu.make_async_copy(whole, whole, link(which, part)).wait()

    if plane:
        all_sent(LINK_X, depth * (rows + half), depth * 2 * packed)
        all_sent(LINK_Y, depth * (rows + half), depth * packed)
    all_sent(LINK_CORE, chips * rows, chips * packed)
    pltpu.make_async_copy(staged, out_hbm, out_sem.at[0]).wait()


def per_device(dims, wrap, activations, out_grads, value_weight, basis_in, basis_out, doc_lengths, queries):
    docs, length, model = activations.shape
    tokens = docs * length
    inner = out_grads.shape[2]
    rank = basis_in.shape[1]
    chips = dims[0] * dims[1] * dims[2]
    reach = dims[0] // 2 + 1 if wrap else dims[0]
    all_docs = 2 * chips * docs
    per_doc = rank // 2
    hbm = pl.BlockSpec(memory_space=pl.ANY)
    input_grad, scores = pl.pallas_call(
        functools.partial(kernel, dims, wrap),
        out_shape=(
            jax.ShapeDtypeStruct((tokens, model), jnp.bfloat16),
            jax.ShapeDtypeStruct((queries.shape[0], all_docs), jnp.float32),
        ),
        in_specs=[pl.BlockSpec(memory_space=pltpu.SMEM)] + [hbm] * 6,
        out_specs=(hbm, pl.BlockSpec(memory_space=pltpu.VMEM)),
        scratch_shapes=[
            pltpu.VMEM((model, inner), jnp.bfloat16),
            pltpu.VMEM((all_docs * per_doc, 2 * rank), jnp.bfloat16),
            pltpu.VMEM((tokens, model), jnp.bfloat16),
            pltpu.VMEM((tokens, inner), jnp.bfloat16),
            pltpu.VMEM((model, rank), jnp.bfloat16),
            pltpu.VMEM((inner, rank), jnp.bfloat16),
            pltpu.VMEM(queries.shape, jnp.bfloat16),
            pltpu.VMEM((tokens, model), jnp.bfloat16),
            pltpu.VMEM((rank, 2 * rank), jnp.float32),
            pltpu.VMEM((all_docs * per_doc, 2 * rank), jnp.float32),
            pltpu.VMEM((all_docs, rank * rank), jnp.bfloat16),
            pltpu.SemaphoreType.DMA((6,)),
            pltpu.SemaphoreType.DMA((2 * chips * PARTS,)),
            pltpu.SemaphoreType.DMA((2 * reach * PARTS,)),
            pltpu.SemaphoreType.DMA((6,)),
            pltpu.SemaphoreType.DMA((1,)),
        ],
        compiler_params=pltpu.CompilerParams(
            collective_id=0, has_side_effects=True, vmem_limit_bytes=40 * 1024 * 1024
        ),
        cost_estimate=pl.CostEstimate(
            flops=2 * tokens * inner * model, bytes_accessed=4 * tokens * model, transcendentals=0
        ),
    )(
        doc_lengths,
        activations.reshape(tokens, model),
        out_grads.reshape(tokens, inner),
        value_weight,
        basis_in,
        basis_out,
        queries,
    )
    return input_grad.reshape(docs, length, model), scores


def solution(mesh):
    placed = (
        P(("group", "shard"), None, None),
        P(("group", "shard"), None, None),
        P("shard", None),
        P(),
        P(),
        P(("group", "shard")),
        P("shard", None),
    )
    shards = mesh.shape["shard"]
    if mesh.shape["group"] == 1 and shards % 8 == 0:
        dims, wrap = (shards // 8, 2, 2), False
    else:
        dims, wrap = (shards // 2, 1, 1), True
    return jax.shard_map(
        functools.partial(per_device, dims, wrap),
        mesh=mesh,
        in_specs=placed,
        out_specs=(P(("group", "shard"), None, None), P("shard", "group")),
        check_vma=False,
    )
```

```python
import functools

import jax
import jax.numpy as jnp
from jax import lax
from jax.experimental import pallas as pl
from jax.experimental.pallas import tpu as pltpu
from jax.sharding import PartitionSpec as P

LINK_X, LINK_Y, LINK_CORE = 0, 1, 2
PARTS = 3


def times(a, b):
    return lax.dot_general(a, b, (((1,), (1,)), ((), ())), preferred_element_type=jnp.float32)


def kernel(
    dims, wrap, lengths, act_hbm, grads_hbm, own_hbm, basis_in_hbm, basis_out_hbm, queries_hbm,
    out_hbm, scores_ref,
    weight, projected, act, grads, basis_in, basis_out, queries, staged, gram, wide, flat,
    load_sem, recv_sem, along_sem, diagonal_sem, link_sem, out_sem,
):
    depth, height, width = dims
    chips = depth * height * width
    me = lax.axis_index("shard")
    core = lax.rem(me, 2)
    x = lax.rem(lax.div(me, 2), width)
    y = lax.rem(lax.div(me, 2 * width), height)
    z = lax.div(me, 2 * width * height)
    rows = own_hbm.shape[0]
    half = rows // 2
    docs = lengths.shape[0]
    length = grads.shape[0] // docs
    rank = basis_in.shape[0]
    packed = projected.shape[0] // (2 * chips)
    per_doc = packed // docs
    plane = width > 1
    reach = depth // 2 + 1 if wrap else depth

    def index(at_z, at_y, at_x, at_core):
        return ((at_z * height + at_y) * width + at_x) * 2 + at_core

    def device(shard):
        return {"shard": shard}

    sibling = index(z, y, x, 1 - core)
    beside_x = index(z, y, 1 - x, core) if plane else None
    beside_y = index(z, 1 - y, x, core) if plane else None

    def at(side, far):
        return lax.rem(z + side * far + depth, depth) if wrap else z + side * far

    def exists(side, far):
        if wrap:
            last = depth // 2 if side > 0 else (depth - 1) // 2
            return (far >= (0 if side > 0 else 1)) & (far <= last)
        if side > 0:
            return (far >= 0) & (z + far < depth)
        return (far >= 1) & (z - far >= 0)

    def goes_on(side, far):
        if wrap:
            return far + 1 <= (depth // 2 if side > 0 else (depth - 1) // 2)
        return z > 0 if side > 0 else z < depth - 1

    special = depth // 2
    at_end = (z == 0) | (z == depth - 1)

    def in_plane(far):
        return (far == 0) | (at_end & (far == special))

    def diagonal_goes_on(side, far):
        to_end = z - 1 == 0 if side > 0 else z + 1 == depth - 1
        return goes_on(side, far) & jnp.logical_not(to_end & (far + 1 == special))

    def place(shard, part):
        if part == 2:
            return projected.at[pl.ds(pl.multiple_of(shard * packed, packed), packed)]
        return weight.at[pl.ds(pl.multiple_of(shard * rows + part * half, half), half)]

    def copy(shard, part, to, send_sem, source=None):
        target = place(shard, part)
        return pltpu.make_async_remote_copy(
            src_ref=target if source is None else source,
            dst_ref=target,
            send_sem=send_sem,
            recv_sem=recv_sem.at[shard * PARTS + part],
            device_id=device(to),
            device_id_type=pl.DeviceIdType.MESH,
        )

    def link(which, part):
        return link_sem.at[which * 2 + (1 if part == 2 else 0)]

    def arrived(shard, part):
        copy(shard, part, sibling, link(LINK_CORE, part)).wait_recv()

    def along(side, far, part):
        return along_sem.at[((0 if side > 0 else 1) * reach + far) * PARTS + part]

    def send_along(side, far, shard, part, source=None):
        @pl.when(goes_on(side, far))
        def _():
            copy(shard, part, index(at(-side, 1), y, x, core), along(side, far, part), source).start()

    def diagonal(side, far, part):
        return diagonal_sem.at[((0 if side > 0 else 1) * reach + far) * PARTS + part]

    def send_diagonal(side, far, shard, part):
        @pl.when(diagonal_goes_on(side, far))
        def _():
            copy(shard, part, index(at(-side, 1), y, x, core), diagonal(side, far, part)).start()

    def send_x(shard, part, source=None):
        if plane:
            copy(shard, part, beside_x, link(LINK_X, part), source).start()

    def send_y(shard, part, source=None):
        if plane:
            copy(shard, part, beside_y, link(LINK_Y, part), source).start()

    def send_core(shard, part, source=None):
        copy(shard, part, sibling, link(LINK_CORE, part), source).start()

    own = weight.at[pl.ds(pl.multiple_of(me * rows, rows), rows)]
    loads = [
        pltpu.make_async_copy(source, target, load_sem.at[i])
        for i, (source, target) in enumerate(
            [
                (grads_hbm, grads),
                (basis_out_hbm, basis_out),
                (basis_in_hbm, basis_in),
                (act_hbm, act),
                (own_hbm, own),
                (queries_hbm, queries),
            ]
        )
    ]
    for load in loads:
        load.start()

    barrier = pltpu.get_barrier_semaphore()

    def greet(other):
        pl.semaphore_signal(barrier, inc=1, device_id=device(other), device_id_type=pl.DeviceIdType.MESH)

    greet(sibling)
    if plane:
        greet(beside_x)
        greet(beside_y)
    partners = 3 if plane else 1
    if wrap:
        greet(index(at(1, 1), y, x, core))
        greet(index(at(-1, 1), y, x, core))
        pl.semaphore_wait(barrier, partners + 2)
    else:
        @pl.when(z + 1 < depth)
        def _():
            greet(index(z + 1, y, x, core))

        @pl.when(z > 0)
        def _():
            greet(index(z - 1, y, x, core))

        pl.semaphore_wait(
            barrier, partners + jnp.where(z + 1 < depth, 1, 0) + jnp.where(z > 0, 1, 0)
        )

    for part in range(2):
        source = own_hbm.at[pl.ds(part * half, half)]
        for side in (1, -1):
            send_along(side, 0, me, part, source)
        send_x(me, part, source)
        send_y(me, part, source)
        send_core(me, part, source)

    for load in loads[:4]:
        load.wait()

    @pl.loop(0, docs)
    def _(doc):
        tokens = pl.ds(pl.multiple_of(doc * length, length), length)
        token = lax.broadcasted_iota(jnp.int32, (length, grads.shape[1]), 0)
        valid = (token < lengths[doc]).astype(jnp.float32)
        grads[tokens, :] = (grads[tokens, :].astype(jnp.float32) * valid).astype(jnp.bfloat16)
        reduced_in = times(act[tokens, :], basis_in[...]).astype(jnp.bfloat16)
        reduced_out = times(grads[tokens, :], basis_out[...])
        both = jnp.concatenate([reduced_out, reduced_out], axis=1).astype(jnp.bfloat16)
        gram[...] = lax.dot_general(
            reduced_in, both, (((0,), (0,)), ((), ())), preferred_element_type=jnp.float32
        )
        even = gram[pl.ds(0, per_doc, stride=2), :]
        odd = gram[pl.ds(1, per_doc, stride=2), :]
        lane = lax.broadcasted_iota(jnp.int32, (per_doc, 2 * rank), 1)
        projected[pl.ds(pl.multiple_of(me * packed + doc * per_doc, per_doc), per_doc), :] = (
            jnp.where(lane < rank, even, odd).astype(jnp.bfloat16)
        )

    for side in (1, -1):
        send_along(side, 0, me, 2)
    send_x(me, 2)
    send_y(me, 2)
    send_core(me, 2)
    loads[4].wait()
    loads[5].wait()

    def pass_on(step, part):
        for side in (1, -1):
            @pl.when(exists(side, step))
            def _(side=side):
                shard = index(at(side, step), y, x, core)
                arrived(shard, part)
                send_along(side, step, shard, part)
                send_x(shard, part)
                send_y(shard, part)
                send_core(shard, part)

            if plane:
                @pl.when(exists(side, step - 1))
                def _(side=side):
                    level = at(side, step - 1)
                    shard = index(level, y, 1 - x, core)
                    arrived(shard, part)
                    if part == 1:
                        pl.when(in_plane(step - 1))(lambda: send_y(shard, part))
                    send_core(shard, part)
                    other = index(level, 1 - y, x, core)
                    arrived(other, part)
                    if part != 1:
                        pl.when(in_plane(step - 1))(lambda: send_x(other, part))
                    send_core(other, part)

                @pl.when(exists(side, step - 2))
                def _(side=side):
                    shard = index(at(side, step - 2), 1 - y, 1 - x, core)
                    arrived(shard, part)
                    send_diagonal(side, step - 2, shard, part)
                    if side > 0:
                        pl.when(step == 2)(lambda: send_diagonal(-1, 0, shard, part))
                    send_core(shard, part)

    def multiply(chip):
        for part in range(2):
            arrived(chip * 2 + 1 - core, part)
        block = weight[pl.ds(pl.multiple_of(chip * 2 * rows, 2 * rows), 2 * rows), :]
        columns = pl.ds(pl.multiple_of(chip * 2 * rows, 2 * rows), 2 * rows)
        staged[:, columns] = times(grads[...], block).astype(jnp.bfloat16)
        pltpu.make_async_copy(staged.at[:, columns], out_hbm.at[:, columns], out_sem.at[0]).start()

    def work(step, first, stop):
        @pl.loop(2 * first, 2 * stop)
        def _(turn):
            column = lax.div(turn, 2)
            turned = lax.rem(turn, 2)
            off_x = lax.rem(column, 2) if plane else 0
            off_y = lax.div(column, 2) if plane else 0
            far = step - 1 - off_x - off_y
            up = exists(1, far) & (turned == 0)
            down = exists(-1, far) & (turned == 1)
            at_x = x + off_x - 2 * x * off_x
            at_y = y + off_y - 2 * y * off_y
            level = at(1 - 2 * turned, far)

            @pl.when(up | down)
            def _():
                multiply((level * height + at_y) * width + at_x)

    last = reach - 1 + (2 if plane else 0)
    columns_of = height * width

    @pl.loop(1, last + 1)
    def _(step):
        pass_on(step, 0)
        work(step, 0, columns_of // 2)
        pass_on(step, 1)
        pass_on(step, 2)
        work(step, columns_of // 2, columns_of)

    @pl.loop(0, chips)
    def _(chip):
        arrived(chip * 2 + 1 - core, 2)

    wide[...] = projected[...].astype(jnp.float32)
    for k in range(per_doc):
        flat[:, k * 2 * rank : (k + 1) * 2 * rank] = wide[
            pl.ds(k, 2 * chips * docs, stride=per_doc), :
        ].astype(jnp.bfloat16)
    scores_ref[...] = times(queries[...], flat[...])
    work(last + 1, 0, columns_of)

    for side in (1, -1):
        @pl.loop(0, reach)
        def _(far, side=side):
            @pl.when((exists(side, far) | (far == 0)) & goes_on(side, far))
            def _():
                shard = index(at(side, far), y, x, core)
                for part in range(PARTS):
                    copy(shard, part, sibling, along(side, far, part)).wait_send()

            if plane:
                @pl.when((exists(side, far) | (far == 0)) & diagonal_goes_on(side, far))
                def _():
                    shard = index(at(side, far), 1 - y, 1 - x, core)
                    for part in range(PARTS):
                        copy(shard, part, sibling, diagonal(side, far, part)).wait_send()

    def all_sent(which, weight_rows, packed_rows):
        for part, ref, size in ((0, weight, weight_rows), (2, projected, packed_rows)):
            whole = ref.at[pl.ds(0, size)]
            pltpu.make_async_copy(whole, whole, link(which, part)).wait()

    if plane:
        for several, extra in ((jnp.logical_not(at_end), 1), (at_end, 2 if depth > 1 else 1)):
            @pl.when(several)
            def _(extra=extra):
                all_sent(LINK_X, depth * rows + extra * half, (depth + extra) * packed)
                all_sent(LINK_Y, depth * rows + extra * half, depth * packed)

    all_sent(LINK_CORE, chips * rows, chips * packed)
    pltpu.make_async_copy(staged, out_hbm, out_sem.at[0]).wait()


def per_device(dims, wrap, activations, out_grads, value_weight, basis_in, basis_out, doc_lengths, queries):
    docs, length, model = activations.shape
    tokens = docs * length
    inner = out_grads.shape[2]
    rank = basis_in.shape[1]
    chips = dims[0] * dims[1] * dims[2]
    reach = dims[0] // 2 + 1 if wrap else dims[0]
    all_docs = 2 * chips * docs
    per_doc = rank // 2
    hbm = pl.BlockSpec(memory_space=pltpu.HBM)
    input_grad, scores = pl.pallas_call(
        functools.partial(kernel, dims, wrap),
        out_shape=(
            jax.ShapeDtypeStruct((tokens, model), jnp.bfloat16),
            jax.ShapeDtypeStruct((queries.shape[0], all_docs), jnp.float32),
        ),
        in_specs=[pl.BlockSpec(memory_space=pltpu.SMEM)] + [hbm] * 6,
        out_specs=(pl.BlockSpec(memory_space=pl.ANY), pl.BlockSpec(memory_space=pltpu.VMEM)),
        scratch_shapes=[
            pltpu.VMEM((model, inner), jnp.bfloat16),
            pltpu.VMEM((all_docs * per_doc, 2 * rank), jnp.bfloat16),
            pltpu.VMEM((tokens, model), jnp.bfloat16),
            pltpu.VMEM((tokens, inner), jnp.bfloat16),
            pltpu.VMEM((rank, model), jnp.bfloat16),
            pltpu.VMEM((rank, inner), jnp.bfloat16),
            pltpu.VMEM(queries.shape, jnp.bfloat16),
            pltpu.VMEM((tokens, model), jnp.bfloat16),
            pltpu.VMEM((rank, 2 * rank), jnp.float32),
            pltpu.VMEM((all_docs * per_doc, 2 * rank), jnp.float32),
            pltpu.VMEM((all_docs, rank * rank), jnp.bfloat16),
            pltpu.SemaphoreType.DMA((6,)),
            pltpu.SemaphoreType.DMA((2 * chips * PARTS,)),
            pltpu.SemaphoreType.DMA((2 * reach * PARTS,)),
            pltpu.SemaphoreType.DMA((2 * reach * PARTS,)),
            pltpu.SemaphoreType.DMA((6,)),
            pltpu.SemaphoreType.DMA((1,)),
        ],
        compiler_params=pltpu.CompilerParams(
            collective_id=0, has_side_effects=True, vmem_limit_bytes=60 * 1024 * 1024
        ),
        cost_estimate=pl.CostEstimate(
            flops=2 * tokens * inner * model, bytes_accessed=4 * tokens * model, transcendentals=0
        ),
    )(
        doc_lengths,
        activations.reshape(tokens, model),
        out_grads.reshape(tokens, inner),
        value_weight,
        basis_in.T,
        basis_out.T,
        queries,
    )
    return input_grad.reshape(docs, length, model), scores


def solution(mesh):
    placed = (
        P(("group", "shard"), None, None),
        P(("group", "shard"), None, None),
        P("shard", None),
        P(),
        P(),
        P(("group", "shard")),
        P("shard", None),
    )
    shards = mesh.shape["shard"]
    if mesh.shape["group"] == 1 and shards % 8 == 0:
        dims, wrap = (shards // 8, 2, 2), False
    else:
        dims, wrap = (shards // 2, 1, 1), True
    return jax.shard_map(
        functools.partial(per_device, dims, wrap),
        mesh=mesh,
        in_specs=placed,
        out_specs=(P(("group", "shard"), None, None), P("shard", "group")),
        check_vma=False,
    )
```

```python
import functools

import jax
import jax.numpy as jnp
from jax import lax
from jax.experimental import pallas as pl
from jax.experimental.pallas import tpu as pltpu
from jax.sharding import PartitionSpec as P

LINK_X, LINK_Y, LINK_CORE = 0, 1, 2
ROW_PARTS = 2
PARTS = ROW_PARTS + 1


def times(a, b):
    return lax.dot_general(a, b, (((1,), (1,)), ((), ())), preferred_element_type=jnp.float32)


def kernel(
    dims, wrap, lengths_hbm, act_hbm, grads_hbm, own_hbm, basis_in_hbm, basis_out_hbm, queries_hbm,
    out_ref, scores_ref,
    lengths, weight, projected, act, grads, basis_in, basis_out, queries, gram, wide, flat,
    load_sem, recv_sem, along_sem, diagonal_sem, link_sem,
):
    depth, height, width = dims
    chips = depth * height * width
    me = lax.axis_index("shard")
    core = lax.rem(me, 2)
    x = lax.rem(lax.div(me, 2), width)
    y = lax.rem(lax.div(me, 2 * width), height)
    z = lax.div(me, 2 * width * height)
    rows = own_hbm.shape[0]
    half = rows // 2
    piece = rows // ROW_PARTS
    docs = lengths.shape[0]
    length = grads.shape[0] // docs
    rank = basis_in.shape[0]
    packed = projected.shape[0] // (2 * chips)
    per_doc = packed // docs
    plane = width > 1
    reach = depth // 2 + 1 if wrap else depth

    def index(at_z, at_y, at_x, at_core):
        return ((at_z * height + at_y) * width + at_x) * 2 + at_core

    def device(shard):
        return {"shard": shard}

    sibling = index(z, y, x, 1 - core)
    beside_x = index(z, y, 1 - x, core) if plane else None
    beside_y = index(z, 1 - y, x, core) if plane else None

    def at(side, far):
        return lax.rem(z + side * far + depth, depth) if wrap else z + side * far

    def exists(side, far):
        if wrap:
            last = depth // 2 if side > 0 else (depth - 1) // 2
            return (far >= (0 if side > 0 else 1)) & (far <= last)
        if side > 0:
            return (far >= 0) & (z + far < depth)
        return (far >= 1) & (z - far >= 0)

    def goes_on(side, far):
        if wrap:
            return far + 1 <= (depth // 2 if side > 0 else (depth - 1) // 2)
        return z > 0 if side > 0 else z < depth - 1

    special = depth - 1
    at_end = (z == 0) | (z == depth - 1)

    def in_plane(far):
        return (far == 0) | (at_end & (far == special))

    def diagonal_goes_on(side, far):
        to_end = z - 1 == 0 if side > 0 else z + 1 == depth - 1
        return goes_on(side, far) & jnp.logical_not(to_end & (far + 1 == special))

    def place(shard, part):
        if part == ROW_PARTS:
            return projected.at[pl.ds(pl.multiple_of(shard * packed, packed), packed)]
        return weight.at[pl.ds(pl.multiple_of(shard * rows + part * piece, piece), piece)]

    def copy(shard, part, to, send_sem, source=None):
        target = place(shard, part)
        return pltpu.make_async_remote_copy(
            src_ref=target if source is None else source,
            dst_ref=target,
            send_sem=send_sem,
            recv_sem=recv_sem.at[shard * PARTS + part],
            device_id=device(to),
            device_id_type=pl.DeviceIdType.MESH,
        )

    def link(which, part):
        return link_sem.at[which * 2 + (1 if part == ROW_PARTS else 0)]

    def arrived(shard, part):
        copy(shard, part, sibling, link(LINK_CORE, part)).wait_recv()

    def along(side, far, part):
        return along_sem.at[((0 if side > 0 else 1) * reach + far) * PARTS + part]

    def send_along(side, far, shard, part, source=None):
        @pl.when(goes_on(side, far))
        def _():
            copy(shard, part, index(at(-side, 1), y, x, core), along(side, far, part), source).start()

    def diagonal(side, far, part):
        return diagonal_sem.at[((0 if side > 0 else 1) * reach + far) * PARTS + part]

    def send_diagonal(side, far, shard, part):
        @pl.when(diagonal_goes_on(side, far))
        def _():
            copy(shard, part, index(at(-side, 1), y, x, core), diagonal(side, far, part)).start()

    def send_x(shard, part, source=None):
        if plane:
            copy(shard, part, beside_x, link(LINK_X, part), source).start()

    def send_y(shard, part, source=None):
        if plane:
            copy(shard, part, beside_y, link(LINK_Y, part), source).start()

    def send_core(shard, part, source=None):
        copy(shard, part, sibling, link(LINK_CORE, part), source).start()

    own = weight.at[pl.ds(pl.multiple_of(me * rows, rows), rows)]
    measures = pltpu.make_async_copy(lengths_hbm, lengths, load_sem.at[6])
    measures.start()
    loads = [
        pltpu.make_async_copy(source, target, load_sem.at[i])
        for i, (source, target) in enumerate(
            [
                (grads_hbm, grads),
                (basis_out_hbm, basis_out),
                (basis_in_hbm, basis_in),
                (act_hbm, act),
                (own_hbm, own),
                (queries_hbm, queries),
            ]
        )
    ]
    for load in loads:
        load.start()

    barrier = pltpu.get_barrier_semaphore()

    def greet(other):
        pl.semaphore_signal(barrier, inc=1, device_id=device(other), device_id_type=pl.DeviceIdType.MESH)

    greet(sibling)
    if plane:
        greet(beside_x)
        greet(beside_y)
    partners = 3 if plane else 1
    if wrap:
        greet(index(at(1, 1), y, x, core))
        greet(index(at(-1, 1), y, x, core))
        pl.semaphore_wait(barrier, partners + 2)
    else:
        @pl.when(z + 1 < depth)
        def _():
            greet(index(z + 1, y, x, core))

        @pl.when(z > 0)
        def _():
            greet(index(z - 1, y, x, core))

        pl.semaphore_wait(
            barrier, partners + jnp.where(z + 1 < depth, 1, 0) + jnp.where(z > 0, 1, 0)
        )

    def send_own(part):
        source = own_hbm.at[pl.ds(part * piece, piece)]
        for side in (1, -1):
            send_along(side, 0, me, part, source)
        send_x(me, part, source)
        send_y(me, part, source)
        send_core(me, part, source)

    for part in range(ROW_PARTS // 2):
        send_own(part)

    measures.wait()
    for load in loads[:4]:
        load.wait()

    @pl.loop(0, docs)
    def _(doc):
        tokens = pl.ds(pl.multiple_of(doc * length, length), length)
        token = lax.broadcasted_iota(jnp.int32, (length, grads.shape[1]), 0)
        valid = (token < lengths[doc]).astype(jnp.float32)
        grads[tokens, :] = (grads[tokens, :].astype(jnp.float32) * valid).astype(jnp.bfloat16)
        reduced_in = times(act[tokens, :], basis_in[...]).astype(jnp.bfloat16)
        reduced_out = times(grads[tokens, :], basis_out[...])
        both = jnp.concatenate([reduced_out, reduced_out], axis=1).astype(jnp.bfloat16)
        gram[...] = lax.dot_general(
            reduced_in, both, (((0,), (0,)), ((), ())), preferred_element_type=jnp.float32
        )
        even = gram[pl.ds(0, per_doc, stride=2), :]
        odd = gram[pl.ds(1, per_doc, stride=2), :]
        lane = lax.broadcasted_iota(jnp.int32, (per_doc, 2 * rank), 1)
        projected[pl.ds(pl.multiple_of(me * packed + doc * per_doc, per_doc), per_doc), :] = (
            jnp.where(lane < rank, even, odd).astype(jnp.bfloat16)
        )

        @pl.when(doc == 0)
        def _():
            for part in range(ROW_PARTS // 2, ROW_PARTS):
                send_own(part)

    for side in (1, -1):
        send_along(side, 0, me, ROW_PARTS)
    send_x(me, ROW_PARTS)
    send_y(me, ROW_PARTS)
    send_core(me, ROW_PARTS)
    loads[4].wait()
    loads[5].wait()

    def pass_on(step, part):
        by_y = ROW_PARTS // 2 <= part < ROW_PARTS

        for side in (1, -1):
            @pl.when(exists(side, step))
            def _(side=side):
                shard = index(at(side, step), y, x, core)
                arrived(shard, part)
                send_along(side, step, shard, part)
                send_x(shard, part)
                send_y(shard, part)
                send_core(shard, part)

            if plane:
                @pl.when(exists(side, step - 1))
                def _(side=side):
                    level = at(side, step - 1)
                    shard = index(level, y, 1 - x, core)
                    arrived(shard, part)
                    if by_y:
                        pl.when(in_plane(step - 1))(lambda: send_y(shard, part))
                    send_core(shard, part)
                    other = index(level, 1 - y, x, core)
                    arrived(other, part)
                    if not by_y:
                        pl.when(in_plane(step - 1))(lambda: send_x(other, part))
                    send_core(other, part)

                @pl.when(exists(side, step - 2))
                def _(side=side):
                    shard = index(at(side, step - 2), 1 - y, 1 - x, core)
                    arrived(shard, part)
                    send_diagonal(side, step - 2, shard, part)
                    if side > 0:
                        pl.when(step == 2)(lambda: send_diagonal(-1, 0, shard, part))
                    send_core(shard, part)

    def multiply(chip):
        for part in range(ROW_PARTS):
            arrived(chip * 2 + 1 - core, part)
        block = weight[pl.ds(pl.multiple_of(chip * 2 * rows, 2 * rows), 2 * rows), :]
        columns = pl.ds(pl.multiple_of(chip * 2 * rows, 2 * rows), 2 * rows)
        out_ref[:, columns] = times(grads[...], block).astype(jnp.bfloat16)

    def work(step, first, stop):
        @pl.loop(2 * first, 2 * stop)
        def _(turn):
            column = lax.div(turn, 2)
            turned = lax.rem(turn, 2)
            off_x = lax.rem(column, 2) if plane else 0
            off_y = lax.div(column, 2) if plane else 0
            far = step - 1 - off_x - off_y
            up = exists(1, far) & (turned == 0)
            down = exists(-1, far) & (turned == 1)
            at_x = x + off_x - 2 * x * off_x
            at_y = y + off_y - 2 * y * off_y
            level = at(1 - 2 * turned, far)

            @pl.when(up | down)
            def _():
                multiply((level * height + at_y) * width + at_x)

    last = reach - 1 + (2 if plane else 0)
    columns_of = height * width

    @pl.loop(1, last + 1)
    def _(step):
        for part in range(ROW_PARTS // 2):
            pass_on(step, part)
        work(step, 0, columns_of // 2)
        for part in range(ROW_PARTS // 2, PARTS):
            pass_on(step, part)
        work(step, columns_of // 2, columns_of)

    @pl.loop(0, chips)
    def _(chip):
        arrived(chip * 2 + 1 - core, ROW_PARTS)

    wide[...] = projected[...].astype(jnp.float32)
    for k in range(per_doc):
        flat[:, k * 2 * rank : (k + 1) * 2 * rank] = wide[
            pl.ds(k, 2 * chips * docs, stride=per_doc), :
        ].astype(jnp.bfloat16)
    scores_ref[...] = times(queries[...], flat[...])
    work(last + 1, 0, columns_of)

    for side in (1, -1):
        @pl.loop(0, reach)
        def _(far, side=side):
            @pl.when((exists(side, far) | (far == 0)) & goes_on(side, far))
            def _():
                shard = index(at(side, far), y, x, core)
                for part in range(PARTS):
                    copy(shard, part, sibling, along(side, far, part)).wait_send()

            if plane:
                @pl.when((exists(side, far) | (far == 0)) & diagonal_goes_on(side, far))
                def _():
                    shard = index(at(side, far), 1 - y, 1 - x, core)
                    for part in range(PARTS):
                        copy(shard, part, sibling, diagonal(side, far, part)).wait_send()

    def all_sent(which, weight_rows, packed_rows):
        for part, ref, size in ((0, weight, weight_rows), (ROW_PARTS, projected, packed_rows)):
            whole = ref.at[pl.ds(0, size)]
            pltpu.make_async_copy(whole, whole, link(which, part)).wait()

    if plane:
        for several, extra in ((jnp.logical_not(at_end), 1), (at_end, 2 if depth > 1 else 1)):
            @pl.when(several)
            def _(extra=extra):
                all_sent(LINK_X, depth * rows + extra * half, (depth + extra) * packed)
                all_sent(LINK_Y, depth * rows + extra * half, depth * packed)

    all_sent(LINK_CORE, chips * rows, chips * packed)


def per_device(dims, wrap, activations, out_grads, value_weight, basis_in, basis_out, doc_lengths, queries):
    docs, length, model = activations.shape
    tokens = docs * length
    inner = out_grads.shape[2]
    rank = basis_in.shape[1]
    chips = dims[0] * dims[1] * dims[2]
    reach = dims[0] // 2 + 1 if wrap else dims[0]
    all_docs = 2 * chips * docs
    per_doc = rank // 2
    hbm = pl.BlockSpec(memory_space=pltpu.HBM)
    input_grad, scores = pl.pallas_call(
        functools.partial(kernel, dims, wrap),
        out_shape=(
            pltpu.VMEM((tokens, model), jnp.bfloat16),
            jax.ShapeDtypeStruct((queries.shape[0], all_docs), jnp.float32),
        ),
        in_specs=[hbm] * 7,
        out_specs=(pl.BlockSpec(memory_space=pltpu.VMEM), pl.BlockSpec(memory_space=pltpu.VMEM)),
        scratch_shapes=[
            pltpu.SMEM((docs,), jnp.int32),
            pltpu.VMEM((model, inner), jnp.bfloat16),
            pltpu.VMEM((all_docs * per_doc, 2 * rank), jnp.bfloat16),
            pltpu.VMEM((tokens, model), jnp.bfloat16),
            pltpu.VMEM((tokens, inner), jnp.bfloat16),
            pltpu.VMEM((rank, model), jnp.bfloat16),
            pltpu.VMEM((rank, inner), jnp.bfloat16),
            pltpu.VMEM(queries.shape, jnp.bfloat16),
            pltpu.VMEM((rank, 2 * rank), jnp.float32),
            pltpu.VMEM((all_docs * per_doc, 2 * rank), jnp.float32),
            pltpu.VMEM((all_docs, rank * rank), jnp.bfloat16),
            pltpu.SemaphoreType.DMA((7,)),
            pltpu.SemaphoreType.DMA((2 * chips * PARTS,)),
            pltpu.SemaphoreType.DMA((2 * reach * PARTS,)),
            pltpu.SemaphoreType.DMA((2 * reach * PARTS,)),
            pltpu.SemaphoreType.DMA((6,)),
        ],
        compiler_params=pltpu.CompilerParams(
            collective_id=0, has_side_effects=True, vmem_limit_bytes=40 * 1024 * 1024
        ),
        cost_estimate=pl.CostEstimate(
            flops=2 * tokens * inner * model, bytes_accessed=4 * tokens * model, transcendentals=0
        ),
    )(
        *(
            pltpu.with_memory_space_constraint(a, pltpu.HBM)
            for a in (
                doc_lengths,
                activations.reshape(tokens, model),
                out_grads.reshape(tokens, inner),
                value_weight,
                basis_in.T,
                basis_out.T,
                queries,
            )
        ),
    )
    return input_grad.reshape(docs, length, model), scores


def solution(mesh):
    placed = (
        P(("group", "shard"), None, None),
        P(("group", "shard"), None, None),
        P("shard", None),
        P(),
        P(),
        P(("group", "shard")),
        P("shard", None),
    )
    shards = mesh.shape["shard"]
    if mesh.shape["group"] == 1 and shards % 8 == 0:
        dims, wrap = (shards // 8, 2, 2), False
    else:
        dims, wrap = (shards // 2, 1, 1), True
    return jax.shard_map(
        functools.partial(per_device, dims, wrap),
        mesh=mesh,
        in_specs=placed,
        out_specs=(P(("group", "shard"), None, None), P("shard", "group")),
        check_vma=False,
    )
```

```python
import functools

import jax
import jax.numpy as jnp
from jax import lax
from jax.experimental import pallas as pl
from jax.experimental.pallas import tpu as pltpu
from jax.sharding import PartitionSpec as P

LINK_X, LINK_Y, LINK_CORE = 0, 1, 2
ROW_PARTS = 2
PARTS = ROW_PARTS + 1


def times(a, b):
    return lax.dot_general(a, b, (((1,), (1,)), ((), ())), preferred_element_type=jnp.float32)


def kernel(
    dims, wrap, lengths_hbm, act_hbm, grads_hbm, own_hbm, basis_in_hbm, basis_out_hbm, queries_hbm,
    out_ref, scores_ref,
    lengths, weight, projected, act, grads, basis_in, basis_out, queries, gram, wide, flat,
    load_sem, recv_sem, along_sem, diagonal_sem, link_sem,
):
    depth, height, width = dims
    chips = depth * height * width
    me = lax.axis_index("shard")
    core = lax.rem(me, 2)
    x = lax.rem(lax.div(me, 2), width)
    y = lax.rem(lax.div(me, 2 * width), height)
    z = lax.div(me, 2 * width * height)
    rows = own_hbm.shape[0]
    half = rows // 2
    piece = rows // ROW_PARTS
    docs = lengths.shape[0]
    length = grads.shape[0] // docs
    rank = basis_in.shape[0]
    packed = projected.shape[0] // (2 * chips)
    per_doc = packed // docs
    plane = width > 1
    reach = depth // 2 + 1 if wrap else depth

    def index(at_z, at_y, at_x, at_core):
        return ((at_z * height + at_y) * width + at_x) * 2 + at_core

    def device(shard):
        return {"shard": shard}

    sibling = index(z, y, x, 1 - core)
    beside_x = index(z, y, 1 - x, core) if plane else None
    beside_y = index(z, 1 - y, x, core) if plane else None

    def at(side, far):
        return lax.rem(z + side * far + depth, depth) if wrap else z + side * far

    def exists(side, far):
        if wrap:
            last = depth // 2 if side > 0 else (depth - 1) // 2
            return (far >= (0 if side > 0 else 1)) & (far <= last)
        if side > 0:
            return (far >= 0) & (z + far < depth)
        return (far >= 1) & (z - far >= 0)

    def goes_on(side, far):
        if wrap:
            return far + 1 <= (depth // 2 if side > 0 else (depth - 1) // 2)
        return z > 0 if side > 0 else z < depth - 1

    special = depth - 1
    at_end = (z == 0) | (z == depth - 1)

    def in_plane(far):
        return (far == 0) | (at_end & (far == special))

    def waits(far):
        return at_end & (far >= 1) & (far < depth - 1)

    def diagonal_goes_on(side, far):
        to_end = z - 1 == 0 if side > 0 else z + 1 == depth - 1
        return goes_on(side, far) & jnp.logical_not(to_end & (far + 1 == special))

    def place(shard, part):
        if part == ROW_PARTS:
            return projected.at[pl.ds(pl.multiple_of(shard * packed, packed), packed)]
        return weight.at[pl.ds(pl.multiple_of(shard * rows + part * piece, piece), piece)]

    def copy(shard, part, to, send_sem, source=None):
        target = place(shard, part)
        return pltpu.make_async_remote_copy(
            src_ref=target if source is None else source,
            dst_ref=target,
            send_sem=send_sem,
            recv_sem=recv_sem.at[shard * PARTS + part],
            device_id=device(to),
            device_id_type=pl.DeviceIdType.MESH,
        )

    def link(which, part):
        return link_sem.at[which * 2 + (1 if part == ROW_PARTS else 0)]

    def arrived(shard, part):
        copy(shard, part, sibling, link(LINK_CORE, part)).wait_recv()

    def along(side, far, part):
        return along_sem.at[((0 if side > 0 else 1) * reach + far) * PARTS + part]

    def send_along(side, far, shard, part, source=None):
        @pl.when(goes_on(side, far))
        def _():
            copy(shard, part, index(at(-side, 1), y, x, core), along(side, far, part), source).start()

    def diagonal(side, far, part):
        return diagonal_sem.at[((0 if side > 0 else 1) * reach + far) * PARTS + part]

    def send_diagonal(side, far, shard, part):
        @pl.when(diagonal_goes_on(side, far))
        def _():
            copy(shard, part, index(at(-side, 1), y, x, core), diagonal(side, far, part)).start()

    def send_x(shard, part, source=None):
        if plane:
            copy(shard, part, beside_x, link(LINK_X, part), source).start()

    def send_y(shard, part, source=None):
        if plane:
            copy(shard, part, beside_y, link(LINK_Y, part), source).start()

    def send_core(shard, part, source=None):
        copy(shard, part, sibling, link(LINK_CORE, part), source).start()

    barrier = pltpu.get_barrier_semaphore()

    def greet(other):
        pl.semaphore_signal(barrier, inc=1, device_id=device(other), device_id_type=pl.DeviceIdType.MESH)

    greet(sibling)
    if plane:
        greet(beside_x)
        greet(beside_y)
    partners = 3 if plane else 1
    if wrap:
        greet(index(at(1, 1), y, x, core))
        greet(index(at(-1, 1), y, x, core))
        expected = partners + 2
    else:
        @pl.when(z + 1 < depth)
        def _():
            greet(index(z + 1, y, x, core))

        @pl.when(z > 0)
        def _():
            greet(index(z - 1, y, x, core))

        expected = partners + jnp.where(z + 1 < depth, 1, 0) + jnp.where(z > 0, 1, 0)

    own = weight.at[pl.ds(pl.multiple_of(me * rows, rows), rows)]
    measures = pltpu.make_async_copy(lengths_hbm, lengths, load_sem.at[6])
    measures.start()
    loads = [
        pltpu.make_async_copy(source, target, load_sem.at[i])
        for i, (source, target) in enumerate(
            [
                (grads_hbm, grads),
                (basis_out_hbm, basis_out),
                (basis_in_hbm, basis_in),
                (act_hbm, act),
                (own_hbm, own),
                (queries_hbm, queries),
            ]
        )
    ]
    for load in loads:
        load.start()

    pl.semaphore_wait(barrier, expected)

    def send_own(part):
        source = own_hbm.at[pl.ds(part * piece, piece)]
        for side in (1, -1):
            send_along(side, 0, me, part, source)
        send_x(me, part, source)
        send_y(me, part, source)
        send_core(me, part, source)

    for part in range(ROW_PARTS // 2):
        send_own(part)

    measures.wait()
    for load in loads[:4]:
        load.wait()

    @pl.loop(0, docs)
    def _(doc):
        tokens = pl.ds(pl.multiple_of(doc * length, length), length)
        token = lax.broadcasted_iota(jnp.int32, (length, grads.shape[1]), 0)
        valid = (token < lengths[doc]).astype(jnp.float32)
        grads[tokens, :] = (grads[tokens, :].astype(jnp.float32) * valid).astype(jnp.bfloat16)
        reduced_in = times(act[tokens, :], basis_in[...]).astype(jnp.bfloat16)
        reduced_out = times(grads[tokens, :], basis_out[...])
        both = jnp.concatenate([reduced_out, reduced_out], axis=1).astype(jnp.bfloat16)
        gram[...] = lax.dot_general(
            reduced_in, both, (((0,), (0,)), ((), ())), preferred_element_type=jnp.float32
        )
        even = gram[pl.ds(0, per_doc, stride=2), :]
        odd = gram[pl.ds(1, per_doc, stride=2), :]
        lane = lax.broadcasted_iota(jnp.int32, (per_doc, 2 * rank), 1)
        projected[pl.ds(pl.multiple_of(me * packed + doc * per_doc, per_doc), per_doc), :] = (
            jnp.where(lane < rank, even, odd).astype(jnp.bfloat16)
        )

        @pl.when(doc == 0)
        def _():
            for part in range(ROW_PARTS // 2, ROW_PARTS):
                send_own(part)

    for side in (1, -1):
        send_along(side, 0, me, ROW_PARTS)
    send_x(me, ROW_PARTS)
    send_y(me, ROW_PARTS)
    send_core(me, ROW_PARTS)
    loads[4].wait()
    loads[5].wait()

    def pass_on(step, part):
        by_y = ROW_PARTS // 2 <= part < ROW_PARTS

        for side in (1, -1):
            @pl.when(exists(side, step))
            def _(side=side):
                shard = index(at(side, step), y, x, core)
                arrived(shard, part)
                send_along(side, step, shard, part)
                send_x(shard, part)
                send_y(shard, part)
                send_core(shard, part)

            if plane:
                @pl.when(exists(side, step - 1))
                def _(side=side):
                    level = at(side, step - 1)
                    shard = index(level, y, 1 - x, core)
                    arrived(shard, part)
                    if by_y:
                        pl.when(in_plane(step - 1))(lambda: send_y(shard, part))
                    send_core(shard, part)
                    other = index(level, 1 - y, x, core)
                    arrived(other, part)
                    if not by_y:
                        pl.when(in_plane(step - 1))(lambda: send_x(other, part))
                    send_core(other, part)

                @pl.when(exists(side, step - 2) & jnp.logical_not(waits(step - 2)))
                def _(side=side):
                    shard = index(at(side, step - 2), 1 - y, 1 - x, core)
                    arrived(shard, part)
                    send_diagonal(side, step - 2, shard, part)
                    if side > 0:
                        pl.when(step == 2)(lambda: send_diagonal(-1, 0, shard, part))
                    send_core(shard, part)

                @pl.when(exists(side, step - 3) & waits(step - 3))
                def _(side=side):
                    shard = index(at(side, step - 3), 1 - y, 1 - x, core)
                    arrived(shard, part)
                    send_core(shard, part)

    def multiply(chip):
        for part in range(ROW_PARTS):
            arrived(chip * 2 + 1 - core, part)
        block = weight[pl.ds(pl.multiple_of(chip * 2 * rows, 2 * rows), 2 * rows), :]
        columns = pl.ds(pl.multiple_of(chip * 2 * rows, 2 * rows), 2 * rows)
        out_ref[:, columns] = times(grads[...], block).astype(jnp.bfloat16)

    def work(step, first, stop):
        @pl.loop(2 * first, 2 * stop)
        def _(turn):
            column = lax.div(turn, 2)
            turned = lax.rem(turn, 2)
            off_x = lax.rem(column, 2) if plane else 0
            off_y = lax.div(column, 2) if plane else 0
            far = step - 1 - off_x - off_y
            up = exists(1, far) & (turned == 0)
            down = exists(-1, far) & (turned == 1)
            at_x = x + off_x - 2 * x * off_x
            at_y = y + off_y - 2 * y * off_y
            level = at(1 - 2 * turned, far)

            @pl.when(up | down)
            def _():
                multiply((level * height + at_y) * width + at_x)

    last = reach - 1 + (2 if plane else 0)
    columns_of = height * width

    @pl.loop(1, last + 1)
    def _(step):
        for part in range(ROW_PARTS // 2):
            pass_on(step, part)
        work(step, 0, columns_of // 2)
        for part in range(ROW_PARTS // 2, PARTS):
            pass_on(step, part)
        work(step, columns_of // 2, columns_of)

    @pl.loop(0, chips)
    def _(chip):
        arrived(chip * 2 + 1 - core, ROW_PARTS)

    wide[...] = projected[...].astype(jnp.float32)
    for k in range(per_doc):
        flat[:, k * 2 * rank : (k + 1) * 2 * rank] = wide[
            pl.ds(k, 2 * chips * docs, stride=per_doc), :
        ].astype(jnp.bfloat16)
    scores_ref[...] = times(queries[...], flat[...])
    work(last + 1, 0, columns_of)

    for side in (1, -1):
        @pl.loop(0, reach)
        def _(far, side=side):
            @pl.when((exists(side, far) | (far == 0)) & goes_on(side, far))
            def _():
                shard = index(at(side, far), y, x, core)
                for part in range(PARTS):
                    copy(shard, part, sibling, along(side, far, part)).wait_send()

            if plane:
                @pl.when((exists(side, far) | (far == 0)) & diagonal_goes_on(side, far))
                def _():
                    shard = index(at(side, far), 1 - y, 1 - x, core)
                    for part in range(PARTS):
                        copy(shard, part, sibling, diagonal(side, far, part)).wait_send()

    def all_sent(which, weight_rows, packed_rows):
        for part, ref, size in ((0, weight, weight_rows), (ROW_PARTS, projected, packed_rows)):
            whole = ref.at[pl.ds(0, size)]
            pltpu.make_async_copy(whole, whole, link(which, part)).wait()

    if plane:
        for several, extra in ((jnp.logical_not(at_end), 1), (at_end, 2 if depth > 1 else 1)):
            @pl.when(several)
            def _(extra=extra):
                all_sent(LINK_X, depth * rows + extra * half, (depth + extra) * packed)
                all_sent(LINK_Y, depth * rows + extra * half, depth * packed)

    all_sent(LINK_CORE, chips * rows, chips * packed)


def per_device(dims, wrap, activations, out_grads, value_weight, basis_in, basis_out, doc_lengths, queries):
    docs, length, model = activations.shape
    tokens = docs * length
    inner = out_grads.shape[2]
    rank = basis_in.shape[1]
    chips = dims[0] * dims[1] * dims[2]
    reach = dims[0] // 2 + 1 if wrap else dims[0]
    all_docs = 2 * chips * docs
    per_doc = rank // 2
    hbm = pl.BlockSpec(memory_space=pltpu.HBM)
    input_grad, scores = pl.pallas_call(
        functools.partial(kernel, dims, wrap),
        out_shape=(
            pltpu.VMEM((tokens, model), jnp.bfloat16),
            jax.ShapeDtypeStruct((queries.shape[0], all_docs), jnp.float32),
        ),
        in_specs=[hbm] * 7,
        out_specs=(pl.BlockSpec(memory_space=pltpu.VMEM), pl.BlockSpec(memory_space=pltpu.VMEM)),
        scratch_shapes=[
            pltpu.SMEM((docs,), jnp.int32),
            pltpu.VMEM((model, inner), jnp.bfloat16),
            pltpu.VMEM((all_docs * per_doc, 2 * rank), jnp.bfloat16),
            pltpu.VMEM((tokens, model), jnp.bfloat16),
            pltpu.VMEM((tokens, inner), jnp.bfloat16),
            pltpu.VMEM((rank, model), jnp.bfloat16),
            pltpu.VMEM((rank, inner), jnp.bfloat16),
            pltpu.VMEM(queries.shape, jnp.bfloat16),
            pltpu.VMEM((rank, 2 * rank), jnp.float32),
            pltpu.VMEM((all_docs * per_doc, 2 * rank), jnp.float32),
            pltpu.VMEM((all_docs, rank * rank), jnp.bfloat16),
            pltpu.SemaphoreType.DMA((7,)),
            pltpu.SemaphoreType.DMA((2 * chips * PARTS,)),
            pltpu.SemaphoreType.DMA((2 * reach * PARTS,)),
            pltpu.SemaphoreType.DMA((2 * reach * PARTS,)),
            pltpu.SemaphoreType.DMA((6,)),
        ],
        compiler_params=pltpu.CompilerParams(
            collective_id=0, has_side_effects=True, vmem_limit_bytes=40 * 1024 * 1024
        ),
        cost_estimate=pl.CostEstimate(
            flops=2 * tokens * inner * model, bytes_accessed=4 * tokens * model, transcendentals=0
        ),
    )(
        *(
            pltpu.with_memory_space_constraint(a, pltpu.HBM)
            for a in (
                doc_lengths,
                activations.reshape(tokens, model),
                out_grads.reshape(tokens, inner),
                value_weight,
                basis_in.T,
                basis_out.T,
                queries,
            )
        ),
    )
    return input_grad.reshape(docs, length, model), scores


def solution(mesh):
    placed = (
        P(("group", "shard"), None, None),
        P(("group", "shard"), None, None),
        P("shard", None),
        P(),
        P(),
        P(("group", "shard")),
        P("shard", None),
    )
    shards = mesh.shape["shard"]
    if mesh.shape["group"] == 1 and shards % 8 == 0:
        dims, wrap = (shards // 8, 2, 2), False
    else:
        dims, wrap = (shards // 2, 1, 1), True
    return jax.shard_map(
        functools.partial(per_device, dims, wrap),
        mesh=mesh,
        in_specs=placed,
        out_specs=(P(("group", "shard"), None, None), P("shard", "group")),
        check_vma=False,
    )
```
